256 devices in a mesh: tok: 8 (over y_lo, x), voc: 32 (over y_hi, z, core).
Axes of the slice: x: 4, y: 4 (y_hi: 2, y_lo: 2; y = y_hi * 2 + y_lo), z: 8, core: 2. Of those that a mesh axis runs over, the one named last changes fastest.
Arguments:
- hidden: bfloat16 [2944, 4096], P('tok'), may hold values from -240 to 240
- head_weight: bfloat16 [4096, 77824], P('tok', 'voc'), may hold values from -0.375 to 0.375
- teacher_scores: float32 [1472, 155648], P('tok', 'voc'), may hold values from -40 to 450
- token_ids: int32 [2944], P('tok'), may hold values from 0 to 77823
Outputs:
- hidden_grad: bfloat16 [2944, 4096], P('tok', 'voc')
The draws below stay inside these ranges and needn't reach their ends.
All inputs are finite; a program needn't handle non-finite values.
Results may differ from the reference program's by a relative error of at most 0.0041.
Values may be sent and summed in bfloat16 or wider, within the bound.
No kernel may reach another device: no remote copies, remote signals or barrier semaphores. Data moves between devices by JAX's collectives and lax.ppermute only.
A program may use at most 128 MiB of HBM per device.

```python
import jax
import jax.numpy as jnp
from jax import lax

D = 4096
VS = 2432
TOK_DEV = 368
V = 77824
TOKENS = 2944
N_TOK = 8
N_VOC = 32


def draw_hidden(key, part):
    key = jax.random.fold_in(key, 11)
    first_key = jax.random.fold_in(key, 0)
    values = jnp.clip(jax.random.normal(first_key, (TOKENS, D), jnp.float32), -6.0, 6.0)
    return values.astype(jnp.bfloat16)


def draw_teacher_scores(key, part):
    key = jax.random.fold_in(key, 23)
    first_key = jax.random.fold_in(key, 0)
    values = 6.0 * jnp.clip(jax.random.normal(first_key, (TOKENS // 2, 2 * V), jnp.float32), -6.0, 6.0)
    return values


def set_ends(array, key, smallest, high):
    spot = [jax.random.randint(jax.random.fold_in(key, axis), (), 0, length) for axis, length in enumerate(array.shape)]
    longest = array.shape.index(max(array.shape))
    neighbour = spot[:longest] + [(spot[longest] + 1) % array.shape[longest]] + spot[longest + 1:]
    return array.at[tuple(spot)].set(smallest).at[tuple(neighbour)].set(high)


def shard_levels(rng, dims, shards, smallest, high):
    factor_of, own = 1.0, jax.random.fold_in(rng, 6)
    for position, blocks in shards:
        draws = jnp.exp(jax.random.uniform(jax.random.fold_in(own, position), (blocks,), jnp.float32, smallest / len(shards), high / len(shards)))
        factor_of = factor_of * jnp.repeat(draws, dims[position] // blocks).reshape([-1 if axis == position else 1 for axis in range(len(dims))])
    return factor_of


def bell_draw(stream_key, extent, scale, bound, pieces=(), held_as=jnp.bfloat16):
    array = jax.random.normal(stream_key, extent, jnp.float32) * scale
    if len(pieces) > 0:
        array = shard_levels(stream_key, extent, pieces, -0.22, 0.18) * array
    return jnp.clip(array, min=-bound, max=bound).astype(held_as)


def setup_inputs(seed: int = 0) -> dict:
    seeds = jax.random.split(jax.random.key(seed), 5)
    hidden = draw_hidden(jax.random.fold_in(seeds[4], 71), 0)
    head_weight = bell_draw(seeds[1], (D, V), (D // 16) ** -0.5, 0.375, ((0, 8), (1, 32)))
    teacher_scores = draw_teacher_scores(jax.random.fold_in(seeds[4], 71), 0)
    token_ids = set_ends(jax.random.randint(seeds[3], (TOKENS,), 0, V), jax.random.fold_in(seeds[3], 1), 0, V - 1).astype(jnp.int32)
    return {"hidden": hidden, "head_weight": head_weight, "teacher_scores": teacher_scores, "token_ids": token_ids}


LOSS_SCALE = 32.0
CE_WEIGHT = 0.5


def reference(hidden, head_weight, teacher_scores, token_ids):
    sectioned = teacher_scores.reshape(N_TOK, TOK_DEV // 2, N_VOC // 2, 2, 2 * VS)
    teacher = sectioned.transpose(0, 3, 1, 2, 4).reshape(N_TOK, TOK_DEV, V)
    blocks = hidden.reshape(N_TOK, TOK_DEV, D)
    id_blocks = token_ids.reshape(N_TOK, TOK_DEV)

    def one_block(items):
        rows, scores, sampled = items
        logits = jnp.dot(rows, head_weight, preferred_element_type=jnp.float32)
        student_gap = logits - jnp.max(logits, axis=1, keepdims=True)
        tempered = jnp.exp(0.5 * student_gap)
        tempered = tempered / jnp.sum(tempered, axis=1, keepdims=True)
        untempered = jnp.exp(student_gap)
        untempered = untempered / jnp.sum(untempered, axis=1, keepdims=True)
        target = jnp.exp(0.5 * (scores - jnp.max(scores, axis=1, keepdims=True)))
        target = target / jnp.sum(target, axis=1, keepdims=True)
        columns = jnp.arange(V, dtype=jnp.int32)[None, :]
        onehot = (columns == sampled[:, None]).astype(jnp.float32)
        grad_logits = (LOSS_SCALE * (2.0 * (tempered - target) + CE_WEIGHT * (untempered - onehot))).astype(jnp.bfloat16)
        result = lax.dot_general(grad_logits, head_weight, (((1,), (1,)), ((), ())), preferred_element_type=jnp.float32)
        return result.astype(jnp.bfloat16)

    out_blocks = lax.map(one_block, (blocks, teacher, id_blocks))
    return out_blocks.reshape(TOKENS, D)
```

```python
import jax
import jax.numpy as jnp
from jax import lax
from jax.experimental import pallas as pl
from jax.experimental.pallas import tpu as pltpu
from jax.sharding import PartitionSpec as P

LOSS_SCALE = 32.0
CE_WEIGHT = 0.5
SEND_SCALE = 512.0
LANES = 128
F32, F16, BF16 = jnp.float32, jnp.float16, jnp.bfloat16
NX, NZ = 4, 8


def x_shift(k):
    return [(i, (i // NX) * NX + (i % NX + k) % NX) for i in range(2 * NX)]


def z_shift(k):
    return [
        (i, (i // (2 * NZ)) * 2 * NZ + (i // 2 % NZ + k) % NZ * 2 + i % 2)
        for i in range(4 * NZ)
    ]


Y_LO = [(i, i ^ NX) for i in range(2 * NX)]
CORE = [(i, i ^ 1) for i in range(4 * NZ)]
Y_HI = [(i, i ^ (2 * NZ)) for i in range(4 * NZ)]
Y_BOTH = [(i, i ^ (NX * 4 * NZ) ^ (2 * NZ)) for i in range(2 * NX * 4 * NZ)]


def tok_move(a, route):
    return lax.ppermute(a, "tok", route)


def voc_move(a, route):
    return lax.ppermute(a, "voc", route)


def both_move(a, route):
    return lax.ppermute(a, ("tok", "voc"), route)


def feature_kernel(place, grad_ref, *refs):
    out_ref = refs[-1]
    shards = refs[:-1]
    core = place[0]
    grad = grad_ref[...]
    step = 0
    for n, pieces in enumerate(SHARD_PIECES):
        rows = []
        for b in range(2):
            if len(pieces) == 1:
                ref, start = shards[pieces[0]], (2 * b + core) * LANES
            else:
                ref, start = shards[pieces[b]], core * LANES
            rows.append(ref[pl.ds(pl.multiple_of(start, LANES), LANES), :])
        block = jnp.concatenate(rows, axis=0)
        part = lax.dot_general(
            grad, block, (((1,), (1,)), ((), ())), preferred_element_type=F32
        )
        at = pl.multiple_of(place[1 + n] * 2 * LANES, 2 * LANES)
        out_ref[:, pl.ds(at, 2 * LANES)] = part.astype(out_ref.dtype)
        step += 1


SHARD_PIECES = ((0,), (1,), (2,), (3, 4), (5,), (6,), (7,), (8, 9))


def feature_part(place, grad, pieces, dtype):
    rows = grad.shape[0]
    columns = 16 * LANES
    whole = pl.BlockSpec(memory_space=pltpu.VMEM)
    return pl.pallas_call(
        feature_kernel,
        out_shape=jax.ShapeDtypeStruct((rows, columns), dtype),
        in_specs=[pl.BlockSpec(memory_space=pltpu.SMEM)] + [whole] * (1 + len(pieces)),
        out_specs=whole,
        compiler_params=pltpu.CompilerParams(vmem_limit_bytes=48 * 1024 * 1024),
        cost_estimate=pl.CostEstimate(
            flops=2 * rows * columns * grad.shape[1],
            bytes_accessed=columns * grad.shape[1] * 4,
            transcendentals=0,
        ),
    )(place, grad, *pieces)


def merge(parts):
    top = parts[0][0]
    for p in parts[1:]:
        top = jnp.maximum(top, p[0])
    out = [top]
    for k in range(1, len(parts[0])):
        power = (0.5, 1.0)[k - 1]
        out.append(sum(p[k] * jnp.exp(power * (p[0] - top)) for p in parts))
    return jnp.stack(out)


def on_device(hidden, head_weight, teacher_scores, token_ids):
    width = head_weight.shape[1]
    tok, voc = lax.axis_index("tok"), lax.axis_index("voc")
    yl, x = tok // NX, tok % NX
    yh, z, core = voc // (2 * NZ), voc // 2 % NZ, voc % 2
    rows = hidden.shape[0]
    half = rows // 2
    part = (width // LANES + 1) // 2 * LANES
    skip = width - part
    overlap = 2 * part - width

    keep = lax.dynamic_slice_in_dim(head_weight, yl * skip, part, 1)
    give = lax.dynamic_slice_in_dim(head_weight, (1 - yl) * skip, part, 1)
    other = tok_move(give, Y_LO)
    k_p, k_m = tok_move(keep, x_shift(1)), tok_move(keep, x_shift(-1))
    hidden_half = lax.dynamic_slice_in_dim(hidden, core * half, half, 0)
    near = tok_move(hidden_half, Y_LO)
    r_p, r_m = tok_move(other, x_shift(1)), tok_move(other, x_shift(-1))
    mid = keep.shape[0] // 2
    fk_p, fk_m = tok_move(k_p[:mid], x_shift(1)), tok_move(k_m[mid:], x_shift(-1))
    fr_p, fr_m = tok_move(r_p[:mid], x_shift(1)), tok_move(r_m[mid:], x_shift(-1))

    far = voc_move(near, CORE)
    first = core == 0
    states = jnp.concatenate(
        [hidden, jnp.where(first, near, far), jnp.where(first, far, near)], axis=0
    )
    ids = jnp.concatenate([token_ids, tok_move(token_ids, Y_LO)])

    top = jnp.max(teacher_scores, axis=1)
    mass = jnp.sum(jnp.exp(0.5 * (teacher_scores - top[:, None])), axis=1)
    seen = jnp.stack([top, mass])
    seen = merge([seen, voc_move(seen, Y_HI)])
    seen = merge([seen, voc_move(seen, z_shift(4))])
    seen = merge([seen] + [voc_move(seen, z_shift(k)) for k in (1, -1, 2)])
    weight = 2.0 * LOSS_SCALE / seen[1]

    def target_block(of_core, of_y):
        block = lax.dynamic_slice_in_dim(
            teacher_scores, of_core * width + of_y * skip, part, 1
        )
        return (jnp.exp(0.5 * (block - seen[0][:, None])) * weight[:, None]).astype(BF16)

    near_t = tok_move(
        jnp.concatenate([target_block(core, 1 - yl), target_block(1 - core, 1 - yl)], 0),
        Y_LO,
    )
    mine_t = [target_block(core, yl), near_t[:half]]
    swap_t = voc_move(jnp.concatenate([target_block(1 - core, yl), near_t[half:]], 0), CORE)
    swap_t = [swap_t[:half], swap_t[half:]]
    target = jnp.concatenate(
        [
            jnp.where(first, a, b)
            for m, s in zip(mine_t, swap_t)
            for a, b in ((m, s), (s, m))
        ],
        axis=0,
    )

    def features(of_y, of_x, start, count):
        at = (of_y * NX + of_x % NX) * 2 * mid + start
        return lax.dynamic_slice_in_dim(states, at, count, 1)

    order = [
        (keep, yl, x, 0),
        (other, 1 - yl, x, 0),
        (k_p, yl, x + 3, 0),
        (k_m, yl, x + 1, 0),
        (r_p, 1 - yl, x + 3, 0),
        (r_m, 1 - yl, x + 1, 0),
        (fk_p, yl, x + 2, 0),
        (fk_m, yl, x + 2, mid),
        (fr_p, 1 - yl, x + 2, 0),
        (fr_m, 1 - yl, x + 2, mid),
    ]
    logits = None
    for piece, of_y, of_x, start in order:
        term = jnp.dot(
            features(of_y, of_x, start, piece.shape[0]), piece, preferred_element_type=F32
        )
        logits = term if logits is None else logits + term

    lane = lax.broadcasted_iota(jnp.int32, logits.shape, 1)
    own = lane >= yl * overlap
    top = jnp.max(jnp.where(own, logits, -jnp.inf), axis=1)
    soft = jnp.where(own, jnp.exp(0.5 * (logits - top[:, None])), 0.0)
    seen = jnp.stack([top, jnp.sum(soft, axis=1), jnp.sum(soft * soft, axis=1)])
    seen = merge([seen, voc_move(seen, CORE)])
    turned = jnp.concatenate([seen[:, rows:], seen[:, :rows]], axis=1)
    seen = merge(
        [seen, tok_move(turned, Y_LO), voc_move(seen, Y_HI), both_move(turned, Y_BOTH)]
    )
    seen = merge([seen, voc_move(seen, z_shift(4))])
    seen = merge([seen] + [voc_move(seen, z_shift(k)) for k in (1, -1, 2)])

    soft = jnp.exp(0.5 * (logits - seen[0][:, None]))
    hit = lane + (voc * width + yl * skip) == ids[:, None]
    grad = (
        soft * (2.0 * LOSS_SCALE / seen[1])[:, None]
        + soft * soft * (CE_WEIGHT * LOSS_SCALE / seen[2])[:, None]
        - target.astype(F32)
        - jnp.where(hit, CE_WEIGHT * LOSS_SCALE, 0.0)
    )
    grad = jnp.where(own, grad, 0.0).astype(BF16)

    pieces = (keep, k_p, k_m, fk_p, fk_m, other, r_p, r_m, fr_p, fr_m)
    slots = [a * NX + (x + k) % NX for a in (yl, 1 - yl) for k in (0, 3, 1, 2)]
    away = feature_part(jnp.stack([1 - core] + slots), grad, pieces, BF16)
    come = voc_move(away, CORE)
    here = feature_part(jnp.stack([core] + slots), grad, pieces, F32)

    def chunk(k):
        at = (z + k) % NZ * LANES
        cols = [(at, LANES), (NZ * LANES + at, LANES)]
        return jnp.concatenate(
            [
                (
                    lax.dynamic_slice_in_dim(here, a, n, 1)
                    + lax.dynamic_slice_in_dim(come, a, n, 1).astype(F32)
                )
                * SEND_SCALE
                for a, n in cols
            ],
            axis=1,
        )

    edge = chunk(4).astype(F16)
    up, down = (
        voc_move(edge[:rows], z_shift(1)),
        voc_move(edge[rows:], z_shift(-1)),
    )
    up = jnp.concatenate([chunk(3)[:rows] + up.astype(F32), chunk(3)[rows:]], 0)
    down = jnp.concatenate([chunk(-3)[:rows], chunk(-3)[rows:] + down.astype(F32)], 0)
    up, down = up.astype(F16), down.astype(F16)
    for k in (2, 1):
        up, down = voc_move(up, z_shift(1)), voc_move(down, z_shift(-1))
        up = (chunk(k) + up.astype(F32)).astype(F16)
        down = (chunk(-k) + down.astype(F32)).astype(F16)
    up, down = voc_move(up, z_shift(1)), voc_move(down, z_shift(-1))
    done = chunk(0) + up.astype(F32) + down.astype(F32)

    def quarter(of_mine, of_yh):
        block = done[:rows] if of_mine else done[rows:]
        return lax.dynamic_slice_in_dim(block, of_yh * LANES, LANES, 1)

    total = (
        quarter(True, yh)
        + tok_move(quarter(False, yh).astype(F16), Y_LO).astype(F32)
        + voc_move(quarter(True, 1 - yh).astype(F16), Y_HI).astype(F32)
        + both_move(quarter(False, 1 - yh).astype(F16), Y_BOTH).astype(F32)
    )
    return (total * (1.0 / SEND_SCALE)).astype(BF16)


def solution(mesh):
    return jax.shard_map(
        on_device,
        mesh=mesh,
        in_specs=(P("tok", None), P("tok", "voc"), P("tok", "voc"), P("tok")),
        out_specs=P("tok", "voc"),
        check_vma=False,
    )
```

```python
import jax
import jax.numpy as jnp
from jax import lax
from jax.experimental import pallas as pl
from jax.experimental.pallas import tpu as pltpu
from jax.sharding import PartitionSpec as P

LOSS_SCALE = 32.0
CE_WEIGHT = 0.5
SEND_SCALE = 512.0
LANES = 128
F32, F16, BF16 = jnp.float32, jnp.float16, jnp.bfloat16
NX, NZ = 4, 8


def x_shift(k):
    return [(i, (i // NX) * NX + (i % NX + k) % NX) for i in range(2 * NX)]


def z_shift(k):
    return [
        (i, (i // (2 * NZ)) * 2 * NZ + (i // 2 % NZ + k) % NZ * 2 + i % 2)
        for i in range(4 * NZ)
    ]


def z_split(k):
    return [pair for way in (k, -k) for pair in z_shift(way) if pair[0] % 2 == (way < 0)]


Y_LO = [(i, i ^ NX) for i in range(2 * NX)]
CORE = [(i, i ^ 1) for i in range(4 * NZ)]
Y_HI = [(i, i ^ (2 * NZ)) for i in range(4 * NZ)]
Y_BOTH = [(i, i ^ (NX * 4 * NZ) ^ (2 * NZ)) for i in range(2 * NX * 4 * NZ)]


def tok_move(a, route):
    return lax.ppermute(a, "tok", route)


def voc_move(a, route):
    return lax.ppermute(a, "voc", route)


def both_move(a, route):
    return lax.ppermute(a, ("tok", "voc"), route)


def merge(parts):
    top = parts[0][0]
    for p in parts[1:]:
        top = jnp.maximum(top, p[0])
    out = [top]
    for k in range(1, len(parts[0])):
        power = (0.5, 1.0)[k - 1]
        out.append(sum(p[k] * jnp.exp(power * (p[0] - top)) for p in parts))
    return jnp.stack(out)


def finish_kernel(hidden_lanes, sum_ref, state_ref, *refs):
    heads, out_ref, seen_ref = refs[:-2], refs[-2], refs[-1]
    logits, at = sum_ref[...], 0
    for head in heads:
        to = at + head.shape[0]
        logits += jnp.dot(state_ref[:, at:to], head[...], preferred_element_type=F32)
        at = to
    out_ref[...] = logits
    own = lax.broadcasted_iota(jnp.int32, logits.shape, 1) >= hidden_lanes[0]
    top = jnp.max(jnp.where(own, logits, -jnp.inf), axis=1, keepdims=True)
    soft = jnp.where(own, jnp.exp(0.5 * (logits - top)), 0.0)
    tempered = jnp.sum(soft, axis=1, keepdims=True)
    plain = jnp.sum(soft * soft, axis=1, keepdims=True)
    lane = lax.broadcasted_iota(jnp.int32, (logits.shape[0], LANES), 1)
    packed = jnp.where(lane == 0, top, jnp.where(lane == 1, tempered, plain))
    seen_ref[0] = packed.T[: seen_ref.shape[1]]


def finish_logits(hidden_lanes, partial, states, heads):
    rows, columns = partial.shape
    block, depth = rows // 2, sum(h.shape[0] for h in heads)
    last = states.shape[1] // depth - 1
    wide = pl.BlockSpec((block, columns), lambda i: (i, 0))
    return pl.pallas_call(
        finish_kernel,
        grid=(2,),
        out_shape=[
            jax.ShapeDtypeStruct((rows, columns), F32),
            jax.ShapeDtypeStruct((2, 8, block), F32),
        ],
        in_specs=[
            pl.BlockSpec(memory_space=pltpu.SMEM),
            wide,
            pl.BlockSpec((block, depth), lambda i: (i, last)),
            *(pl.BlockSpec(h.shape, lambda i: (0, 0)) for h in heads),
        ],
        out_specs=[wide, pl.BlockSpec((1, 8, block), lambda i: (i, 0, 0))],
        compiler_params=pltpu.CompilerParams(vmem_limit_bytes=32 * 1024 * 1024),
        cost_estimate=pl.CostEstimate(
            flops=2 * rows * columns * depth,
            bytes_accessed=8 * rows * columns,
            transcendentals=rows * columns,
        ),
    )(hidden_lanes[None], partial, states, *heads)


def on_device(hidden, head_weight, teacher_scores, token_ids):
    width = head_weight.shape[1]
    tok, voc = lax.axis_index("tok"), lax.axis_index("voc")
    yl, x = tok // NX, tok % NX
    yh, z, core = voc // (2 * NZ), voc // 2 % NZ, voc % 2
    rows = hidden.shape[0]
    half = rows // 2
    part = (width // LANES + 1) // 2 * LANES
    skip = width - part
    overlap = 2 * part - width

    give = lax.dynamic_slice_in_dim(head_weight, (1 - yl) * skip, part, 1)
    other = tok_move(give, Y_LO)
    keep = lax.dynamic_slice_in_dim(head_weight, yl * skip, part, 1)
    k_p, k_m = tok_move(keep, x_shift(1)), tok_move(keep, x_shift(-1))
    r_p, r_m = tok_move(other, x_shift(1)), tok_move(other, x_shift(-1))
    hidden_half = lax.dynamic_slice_in_dim(hidden, core * half, half, 0)
    hidden_half, _ = lax.optimization_barrier((hidden_half, other))
    near = tok_move(hidden_half, Y_LO)
    mid = keep.shape[0] // 2
    far = voc_move(near, CORE)
    on = lax.optimization_barrier((k_p[:mid], k_m[mid:], r_p[:mid], r_m[mid:], near))
    fk_p, fk_m = tok_move(on[0], x_shift(1)), tok_move(on[1], x_shift(-1))
    fr_p, fr_m = tok_move(on[2], x_shift(1)), tok_move(on[3], x_shift(-1))
    first = core == 0

    order = [(a, k) for a in (yl, 1 - yl) for k in (0, 3, 1)] + [(yl, 2), (1 - yl, 2)]

    def arranged(block):
        return jnp.concatenate(
            [
                lax.dynamic_slice_in_dim(block, (a * NX + (x + k) % NX) * 2 * mid, 2 * mid, 1)
                for a, k in order
            ],
            axis=1,
        )

    states = jnp.concatenate(
        [
            arranged(hidden),
            arranged(jnp.where(first, near, far)),
            arranged(jnp.where(first, far, near)),
        ],
        axis=0,
    )

    top = jnp.max(teacher_scores, axis=1)
    mass = jnp.sum(jnp.exp(0.5 * (teacher_scores - top[:, None])), axis=1)

    def teacher_block(of_core, of_y):
        block = lax.dynamic_slice_in_dim(
            teacher_scores, of_core * width + of_y * skip, part, 1
        )
        return jnp.exp(0.5 * (block - top[:, None])).astype(BF16)

    def by_token(mine, swapped, axis):
        return jnp.concatenate(
            [
                jnp.where(first, a, b)
                for m, s in zip(mine, swapped)
                for a, b in ((m, s), (s, m))
            ],
            axis=axis,
        )

    tell = jnp.stack(
        [top, mass, lax.dynamic_slice_in_dim(token_ids, core * half, half, 0).astype(F32)]
    )
    give_t = jnp.concatenate([teacher_block(core, 1 - yl), teacher_block(1 - core, 1 - yl)], 0)
    given, _, _ = lax.optimization_barrier((tell, fk_p, fk_m))
    near_tell = tok_move(given, Y_LO)
    give_t, _ = lax.optimization_barrier((give_t, near_tell))
    near_t = tok_move(give_t, Y_LO)
    told = voc_move(jnp.concatenate([tell, near_tell], 1), CORE)
    told = by_token([tell, near_tell], [told[:, :half], told[:, half:]], 1)
    ids = told[2].astype(jnp.int32)
    swap_t = voc_move(jnp.concatenate([teacher_block(1 - core, yl), near_t[half:]], 0), CORE)
    teacher = by_token(
        [teacher_block(core, yl), near_t[:half]], [swap_t[:half], swap_t[half:]], 0
    )

    early = jnp.concatenate([keep, k_p, k_m, other, r_p, r_m], axis=0)
    logits = jnp.dot(
        states[:, : early.shape[0]], early, preferred_element_type=F32
    )
    def of_core(piece, c):
        groups = piece.reshape(piece.shape[0] // (2 * LANES), 2, LANES, part)
        return lax.dynamic_index_in_dim(groups, c, 1, False).reshape(-1, part)

    def packed(c):
        space = jnp.zeros((4 * LANES, part), BF16)
        return jnp.concatenate([of_core(w, c) for w in (keep, k_p, k_m, other, r_p, r_m)] + [space], 0)

    logits, fk_p, fk_m, fr_p, fr_m, head_far, head_near = lax.optimization_barrier(
        (logits, fk_p, fk_m, fr_p, fr_m, packed(1 - core), packed(core))
    )
    logits, seen = finish_logits(yl * overlap, logits, states, (fk_p, fk_m, fr_p, fr_m))
    late = lax.optimization_barrier((fk_p, fk_m, fr_p, fr_m, seen))[:4]

    def filled(head, c):
        rest = jnp.concatenate([of_core(w, c) for w in late], 0)
        return lax.dynamic_update_slice(head, rest, (head.shape[0] - rest.shape[0], 0))

    head_far = voc_move(filled(head_far, 1 - core), CORE)
    head_near = filled(head_near, core)
    lane = lax.broadcasted_iota(jnp.int32, logits.shape, 1)
    own = lane >= yl * overlap
    seen = jnp.concatenate([seen[0, :3], seen[1, :3]], axis=1)
    seen = merge([seen, voc_move(seen, CORE)])
    turned = jnp.concatenate([seen[:, rows:], seen[:, :rows]], axis=1)
    across = voc_move(jnp.concatenate([seen, told[:2]], 0), Y_HI)
    seen = merge([seen, tok_move(turned, Y_LO), across[:3], both_move(turned, Y_BOTH)])
    seen = jnp.concatenate([seen, merge([told[:2], across[3:]])], 0)

    def merge_all(parts):
        return jnp.concatenate(
            [merge([p[:3] for p in parts]), merge([p[3:] for p in parts])], 0
        )

    one, two = voc_move(seen, z_split(1)), voc_move(seen, z_split(2))
    pair = jnp.where(first, seen, merge_all([seen, one]))
    pair, head_near = lax.optimization_barrier((pair, head_near))
    three = voc_move(pair, z_split(3))
    none = jnp.zeros_like(seen[0])
    blank = jnp.stack([one[0], none, none, one[3], none])
    seen = merge_all([jnp.where(first, seen, blank), one, two, three])
    seen = merge_all([seen, voc_move(seen, CORE)])
    weight = 2.0 * LOSS_SCALE * jnp.exp(0.5 * (told[0] - seen[3])) / seen[4]

    soft = jnp.exp(0.5 * (logits - seen[0][:, None]))
    hit = lane + (voc * width + yl * skip) == ids[:, None]
    grad = (
        soft * (2.0 * LOSS_SCALE / seen[1])[:, None]
        + soft * soft * (CE_WEIGHT * LOSS_SCALE / seen[2])[:, None]
        - teacher.astype(F32) * weight[:, None]
        - jnp.where(hit, CE_WEIGHT * LOSS_SCALE, 0.0)
    )
    grad = jnp.where(own, grad, 0.0).astype(BF16)

    grad_far = voc_move(grad, CORE)

    def back(g, w):
        return lax.dot_general(g, w, (((1,), (1,)), ((), ())), preferred_element_type=F32)

    here = back(grad, head_near)
    grad_far, _ = lax.optimization_barrier((grad_far, here[:8, :LANES]))
    here = here + back(grad_far, head_far)

    def arrival(far_y, dx):
        far_y = far_y.astype(jnp.int32)
        near_x = jnp.where(dx == 0, 0, jnp.where(dx == NX - 1, 1, 2))
        return jnp.where(dx == 2, 6 + far_y, 3 * far_y + near_x)

    def chunk(k):
        to = (z + k) % NZ
        dx = (to // 2 - x) % NX
        cols = [
            (2 * arrival(h != yl, dx) + to % 2) * LANES for h in range(2)
        ]
        return jnp.concatenate(
            [lax.dynamic_slice_in_dim(here, a, LANES, 1) * SEND_SCALE for a in cols], 1
        )

    edge = chunk(4).astype(F16)
    up, down = (
        voc_move(edge[:rows], z_shift(1)),
        voc_move(edge[rows:], z_shift(-1)),
    )
    up = jnp.concatenate([chunk(3)[:rows] + up.astype(F32), chunk(3)[rows:]], 0)
    down = jnp.concatenate([chunk(-3)[:rows], chunk(-3)[rows:] + down.astype(F32)], 0)
    up, down = up.astype(F16), down.astype(F16)
    for k in (2, 1):
        up, down = voc_move(up, z_shift(1)), voc_move(down, z_shift(-1))
        up = (chunk(k) + up.astype(F32)).astype(F16)
        down = (chunk(-k) + down.astype(F32)).astype(F16)
    up, down = voc_move(up, z_shift(1)), voc_move(down, z_shift(-1))
    done = chunk(0) + up.astype(F32) + down.astype(F32)

    def quarter(of_mine, of_yh):
        block = done[:rows] if of_mine else done[rows:]
        return lax.dynamic_slice_in_dim(block, of_yh * LANES, LANES, 1)

    total = (
        quarter(True, yh)
        + tok_move(quarter(False, yh).astype(F16), Y_LO).astype(F32)
        + voc_move(quarter(True, 1 - yh).astype(F16), Y_HI).astype(F32)
        + both_move(quarter(False, 1 - yh).astype(F16), Y_BOTH).astype(F32)
    )
    return (total * (1.0 / SEND_SCALE)).astype(BF16)


def solution(mesh):
    return jax.shard_map(
        on_device,
        mesh=mesh,
        in_specs=(P("tok", None), P("tok", "voc"), P("tok", "voc"), P("tok")),
        out_specs=P("tok", "voc"),
        check_vma=False,
    )
```

```python
import jax
import jax.numpy as jnp
from jax import lax
from jax.experimental import pallas as pl
from jax.experimental.pallas import tpu as pltpu
from jax.sharding import PartitionSpec as P

LOSS_SCALE = 32.0
CE_WEIGHT = 0.5
SEND_SCALE = 512.0
LANES = 128
F32, F16, BF16 = jnp.float32, jnp.float16, jnp.bfloat16
NX, NZ = 4, 8


def x_shift(k):
    return [(i, (i // NX) * NX + (i % NX + k) % NX) for i in range(2 * NX)]


def z_shift(k):
    return [
        (i, (i // (2 * NZ)) * 2 * NZ + (i // 2 % NZ + k) % NZ * 2 + i % 2)
        for i in range(4 * NZ)
    ]


def z_split(k):
    return [pair for way in (k, -k) for pair in z_shift(way) if pair[0] % 2 == (way < 0)]


Y_LO = [(i, i ^ NX) for i in range(2 * NX)]
CORE = [(i, i ^ 1) for i in range(4 * NZ)]
Y_HI = [(i, i ^ (2 * NZ)) for i in range(4 * NZ)]
Y_BOTH = [(i, i ^ (NX * 4 * NZ) ^ (2 * NZ)) for i in range(2 * NX * 4 * NZ)]


def tok_move(a, route):
    return lax.ppermute(a, "tok", route)


def voc_move(a, route):
    return lax.ppermute(a, "voc", route)


def both_move(a, route):
    return lax.ppermute(a, ("tok", "voc"), route)


def merge(parts):
    top = parts[0][0]
    for p in parts[1:]:
        top = jnp.maximum(top, p[0])
    out = [top]
    for k in range(1, len(parts[0])):
        power = (0.5, 1.0)[k - 1]
        out.append(sum(p[k] * jnp.exp(power * (p[0] - top)) for p in parts))
    return jnp.stack(out)


def finish_kernel(hidden_lanes, sum_ref, state_ref, *refs):
    heads, out_ref, seen_ref = refs[:-2], refs[-2], refs[-1]
    logits, at = sum_ref[...], 0
    for head in heads:
        to = at + head.shape[0]
        logits += jnp.dot(state_ref[:, at:to], head[...], preferred_element_type=F32)
        at = to
    out_ref[...] = logits
    own = lax.broadcasted_iota(jnp.int32, logits.shape, 1) >= hidden_lanes[0]
    top = jnp.max(jnp.where(own, logits, -jnp.inf), axis=1, keepdims=True)
    soft = jnp.where(own, jnp.exp(0.5 * (logits - top)), 0.0)
    tempered = jnp.sum(soft, axis=1, keepdims=True)
    plain = jnp.sum(soft * soft, axis=1, keepdims=True)
    lane = lax.broadcasted_iota(jnp.int32, (logits.shape[0], LANES), 1)
    packed = jnp.where(lane == 0, top, jnp.where(lane == 1, tempered, plain))
    seen_ref[0] = packed.T[: seen_ref.shape[1]]


def finish_logits(hidden_lanes, partial, states, up, down):
    rows, columns = partial.shape
    block, depth, mid = rows // 2, 2 * up.shape[0], up.shape[0] // 2
    last = states.shape[1] // depth - 1
    wide = pl.BlockSpec((block, columns), lambda i: (i, 0))
    return pl.pallas_call(
        finish_kernel,
        grid=(2,),
        out_shape=[
            jax.ShapeDtypeStruct((rows, columns), F32),
            jax.ShapeDtypeStruct((2, 8, block), F32),
        ],
        in_specs=[
            pl.BlockSpec(memory_space=pltpu.SMEM),
            wide,
            pl.BlockSpec((block, depth), lambda i: (i, last)),
            *(pl.BlockSpec((mid, columns), lambda i, k=k: (k, 0)) for k in (0, 0, 1, 1)),
        ],
        out_specs=[wide, pl.BlockSpec((1, 8, block), lambda i: (i, 0, 0))],
        compiler_params=pltpu.CompilerParams(vmem_limit_bytes=32 * 1024 * 1024),
        cost_estimate=pl.CostEstimate(
            flops=2 * rows * columns * depth,
            bytes_accessed=8 * rows * columns,
            transcendentals=rows * columns,
        ),
    )(hidden_lanes[None], partial, states, up, down, up, down)


def on_device(hidden, head_weight, teacher_scores, token_ids):
    width = head_weight.shape[1]
    tok, voc = lax.axis_index("tok"), lax.axis_index("voc")
    yl, x = tok // NX, tok % NX
    yh, z, core = voc // (2 * NZ), voc // 2 % NZ, voc % 2
    rows = hidden.shape[0]
    half = rows // 2
    part = (width // LANES + 1) // 2 * LANES
    skip = width - part
    overlap = 2 * part - width

    give = lax.dynamic_slice_in_dim(head_weight, (1 - yl) * skip, part, 1)
    other = tok_move(give, Y_LO)
    keep = lax.dynamic_slice_in_dim(head_weight, yl * skip, part, 1)
    k_p, k_m = tok_move(keep, x_shift(1)), tok_move(keep, x_shift(-1))
    r_p, r_m = tok_move(other, x_shift(1)), tok_move(other, x_shift(-1))
    hidden_half = lax.dynamic_slice_in_dim(hidden, core * half, half, 0)
    hidden_half, _ = lax.optimization_barrier((hidden_half, other))
    near = tok_move(hidden_half, Y_LO)
    mid = keep.shape[0] // 2
    far = voc_move(near, CORE)
    up = jnp.concatenate([k_p[:mid], r_p[:mid]], 0)
    down = jnp.concatenate([k_m[mid:], r_m[mid:]], 0)
    up, down, _ = lax.optimization_barrier((up, down, near))
    up, down = tok_move(up, x_shift(1)), tok_move(down, x_shift(-1))
    first = core == 0

    order = [(a, k) for a in (yl, 1 - yl) for k in (0, 3, 1)] + [(yl, 2), (1 - yl, 2)]

    def arranged(block):
        return jnp.concatenate(
            [
                lax.dynamic_slice_in_dim(block, (a * NX + (x + k) % NX) * 2 * mid, 2 * mid, 1)
                for a, k in order
            ],
            axis=1,
        )

    states = jnp.concatenate(
        [
            arranged(hidden),
            arranged(jnp.where(first, near, far)),
            arranged(jnp.where(first, far, near)),
        ],
        axis=0,
    )

    top = jnp.max(teacher_scores, axis=1)
    mass = jnp.sum(jnp.exp(0.5 * (teacher_scores - top[:, None])), axis=1)

    def teacher_block(of_core, of_y):
        block = lax.dynamic_slice_in_dim(
            teacher_scores, of_core * width + of_y * skip, part, 1
        )
        return jnp.exp(0.5 * (block - top[:, None])).astype(BF16)

    def by_token(mine, swapped, axis):
        return jnp.concatenate(
            [
                jnp.where(first, a, b)
                for m, s in zip(mine, swapped)
                for a, b in ((m, s), (s, m))
            ],
            axis=axis,
        )

    tell = jnp.stack(
        [top, mass, lax.dynamic_slice_in_dim(token_ids, core * half, half, 0).astype(F32)]
    )
    give_t = jnp.concatenate([teacher_block(core, 1 - yl), teacher_block(1 - core, 1 - yl)], 0)
    given, _ = lax.optimization_barrier((tell, far))
    near_tell = tok_move(given, Y_LO)
    give_t, _ = lax.optimization_barrier((give_t, near_tell))
    near_t = tok_move(give_t, Y_LO)
    told = voc_move(jnp.concatenate([tell, near_tell], 1), CORE)
    told = by_token([tell, near_tell], [told[:, :half], told[:, half:]], 1)
    ids = told[2].astype(jnp.int32)
    early = jnp.concatenate([keep, k_p, k_m, other, r_p, r_m], axis=0)
    states, _ = lax.optimization_barrier((states, near_tell))
    logits = jnp.dot(
        states[:, : early.shape[0]], early, preferred_element_type=F32
    )
    def of_core(piece, c):
        groups = piece.reshape(piece.shape[0] // (2 * LANES), 2, LANES, part)
        return lax.dynamic_index_in_dim(groups, c, 1, False).reshape(-1, part)

    def packed(c):
        space = jnp.zeros((4 * LANES, part), BF16)
        return jnp.concatenate([of_core(w, c) for w in (keep, k_p, k_m, other, r_p, r_m)] + [space], 0)

    logits, up, down, head_far, head_near, near_t = lax.optimization_barrier(
        (logits, up, down, packed(1 - core), packed(core), near_t)
    )
    swap_t = voc_move(jnp.concatenate([teacher_block(1 - core, yl), near_t[half:]], 0), CORE)
    teacher = by_token(
        [teacher_block(core, yl), near_t[:half]], [swap_t[:half], swap_t[half:]], 0
    )
    logits, seen = finish_logits(yl * overlap, logits, states, up, down)
    up, down, _ = lax.optimization_barrier((up, down, seen))
    late = (up[:mid], down[:mid], up[mid:], down[mid:])

    def filled(head, c):
        rest = jnp.concatenate([of_core(w, c) for w in late], 0)
        return lax.dynamic_update_slice(head, rest, (head.shape[0] - rest.shape[0], 0))

    head_far = voc_move(filled(head_far, 1 - core), CORE)
    head_near = filled(head_near, core)
    lane = lax.broadcasted_iota(jnp.int32, logits.shape, 1)
    own = lane >= yl * overlap
    seen = jnp.concatenate([seen[0, :3], seen[1, :3]], axis=1)
    seen = merge([seen, voc_move(seen, CORE)])
    turned = jnp.concatenate([seen[:, rows:], seen[:, :rows]], axis=1)
    across = voc_move(jnp.concatenate([seen, told[:2]], 0), Y_HI)
    seen = merge([seen, tok_move(turned, Y_LO), across[:3], both_move(turned, Y_BOTH)])
    seen = jnp.concatenate([seen, merge([told[:2], across[3:]])], 0)

    def merge_all(parts):
        return jnp.concatenate(
            [merge([p[:3] for p in parts]), merge([p[3:] for p in parts])], 0
        )

    one, two = voc_move(seen, z_split(1)), voc_move(seen, z_split(2))
    pair = jnp.where(first, seen, merge_all([seen, one]))
    pair, head_near = lax.optimization_barrier((pair, head_near))
    three = voc_move(pair, z_split(3))
    none = jnp.zeros_like(seen[0])
    blank = jnp.stack([one[0], none, none, one[3], none])
    seen = merge_all([jnp.where(first, seen, blank), one, two, three])
    seen = merge_all([seen, voc_move(seen, CORE)])
    weight = 2.0 * LOSS_SCALE * jnp.exp(0.5 * (told[0] - seen[3])) / seen[4]

    soft = jnp.exp(0.5 * (logits - seen[0][:, None]))
    hit = lane + (voc * width + yl * skip) == ids[:, None]
    grad = (
        soft * (2.0 * LOSS_SCALE / seen[1])[:, None]
        + soft * soft * (CE_WEIGHT * LOSS_SCALE / seen[2])[:, None]
        - teacher.astype(F32) * weight[:, None]
        - jnp.where(hit, CE_WEIGHT * LOSS_SCALE, 0.0)
    )
    grad = jnp.where(own, grad, 0.0).astype(BF16)

    grad_far = voc_move(grad, CORE)

    def back(g, w):
        return lax.dot_general(g, w, (((1,), (1,)), ((), ())), preferred_element_type=F32)

    here = back(grad, head_near)
    grad_far, _ = lax.optimization_barrier((grad_far, here[:8, :LANES]))
    here = here + back(grad_far, head_far)

    def arrival(far_y, dx):
        far_y = far_y.astype(jnp.int32)
        near_x = jnp.where(dx == 0, 0, jnp.where(dx == NX - 1, 1, 2))
        return jnp.where(dx == 2, 6 + far_y, 3 * far_y + near_x)

    def chunk(k):
        to = (z + k) % NZ
        dx = (to // 2 - x) % NX
        cols = [
            (2 * arrival(h != yl, dx) + to % 2) * LANES for h in range(2)
        ]
        return jnp.concatenate(
            [lax.dynamic_slice_in_dim(here, a, LANES, 1) * SEND_SCALE for a in cols], 1
        )

    edge = chunk(4).astype(F16)
    up, down = (
        voc_move(edge[:rows], z_shift(1)),
        voc_move(edge[rows:], z_shift(-1)),
    )
    up = jnp.concatenate([chunk(3)[:rows] + up.astype(F32), chunk(3)[rows:]], 0)
    down = jnp.concatenate([chunk(-3)[:rows], chunk(-3)[rows:] + down.astype(F32)], 0)
    up, down = up.astype(F16), down.astype(F16)
    for k in (2, 1):
        up, down = voc_move(up, z_shift(1)), voc_move(down, z_shift(-1))
        up = (chunk(k) + up.astype(F32)).astype(F16)
        down = (chunk(-k) + down.astype(F32)).astype(F16)
    up, down = voc_move(up, z_shift(1)), voc_move(down, z_shift(-1))
    done = chunk(0) + up.astype(F32) + down.astype(F32)

    def quarter(of_mine, of_yh):
        block = done[:rows] if of_mine else done[rows:]
        return lax.dynamic_slice_in_dim(block, of_yh * LANES, LANES, 1)

    total = (
        quarter(True, yh)
        + tok_move(quarter(False, yh).astype(F16), Y_LO).astype(F32)
        + voc_move(quarter(True, 1 - yh).astype(F16), Y_HI).astype(F32)
        + both_move(quarter(False, 1 - yh).astype(F16), Y_BOTH).astype(F32)
    )
    return (total * (1.0 / SEND_SCALE)).astype(BF16)


def solution(mesh):
    return jax.shard_map(
        on_device,
        mesh=mesh,
        in_specs=(P("tok", None), P("tok", "voc"), P("tok", "voc"), P("tok")),
        out_specs=P("tok", "voc"),
        check_vma=False,
    )
```

```python
import jax
import jax.numpy as jnp
from jax import lax
from jax.experimental import pallas as pl
from jax.experimental.pallas import tpu as pltpu
from jax.sharding import PartitionSpec as P

LOSS_SCALE = 32.0
CE_WEIGHT = 0.5
SEND_SCALE = 512.0
LANES = 128
F32, F16, BF16 = jnp.float32, jnp.float16, jnp.bfloat16
NX, NZ = 4, 8


def x_shift(k):
    return [(i, (i // NX) * NX + (i % NX + k) % NX) for i in range(2 * NX)]


def z_shift(k):
    return [
        (i, (i // (2 * NZ)) * 2 * NZ + (i // 2 % NZ + k) % NZ * 2 + i % 2)
        for i in range(4 * NZ)
    ]


def z_split(k):
    return [pair for way in (k, -k) for pair in z_shift(way) if pair[0] % 2 == (way < 0)]


Y_LO = [(i, i ^ NX) for i in range(2 * NX)]
CORE = [(i, i ^ 1) for i in range(4 * NZ)]
Y_HI = [(i, i ^ (2 * NZ)) for i in range(4 * NZ)]
Y_BOTH = [(i, i ^ (NX * 4 * NZ) ^ (2 * NZ)) for i in range(2 * NX * 4 * NZ)]


def tok_move(a, route):
    return lax.ppermute(a, "tok", route)


def voc_move(a, route):
    return lax.ppermute(a, "voc", route)


def both_move(a, route):
    return lax.ppermute(a, ("tok", "voc"), route)


def merge(parts):
    top = parts[0][0]
    for p in parts[1:]:
        top = jnp.maximum(top, p[0])
    out = [top]
    for k in range(1, len(parts[0])):
        power = (0.5, 1.0)[k - 1]
        out.append(sum(p[k] * jnp.exp(power * (p[0] - top)) for p in parts))
    return jnp.stack(out)


def finish_kernel(hidden_lanes, sum_ref, state_ref, *refs):
    heads, out_ref, seen_ref = refs[:-2], refs[-2], refs[-1]
    logits, at = sum_ref[...], 0
    for head in heads:
        to = at + head.shape[0]
        logits += jnp.dot(state_ref[:, at:to], head[...], preferred_element_type=F32)
        at = to
    out_ref[...] = logits
    own = lax.broadcasted_iota(jnp.int32, logits.shape, 1) >= hidden_lanes[0]
    top = jnp.max(jnp.where(own, logits, -jnp.inf), axis=1, keepdims=True)
    soft = jnp.where(own, jnp.exp(0.5 * (logits - top)), 0.0)
    tempered = jnp.sum(soft, axis=1, keepdims=True)
    plain = jnp.sum(soft * soft, axis=1, keepdims=True)
    lane = lax.broadcasted_iota(jnp.int32, (logits.shape[0], LANES), 1)
    packed = jnp.where(lane == 0, top, jnp.where(lane == 1, tempered, plain))
    seen_ref[0] = packed.T[: seen_ref.shape[1]]


def finish_logits(hidden_lanes, partial, states, up, down):
    rows, columns = partial.shape
    block, depth, mid = rows // 2, 2 * up.shape[0], up.shape[0] // 2
    last = states.shape[1] // depth - 1
    wide = pl.BlockSpec((block, columns), lambda i: (i, 0))
    return pl.pallas_call(
        finish_kernel,
        grid=(2,),
        out_shape=[
            jax.ShapeDtypeStruct((rows, columns), F32),
            jax.ShapeDtypeStruct((2, 8, block), F32),
        ],
        in_specs=[
            pl.BlockSpec(memory_space=pltpu.SMEM),
            wide,
            pl.BlockSpec((block, depth), lambda i: (i, last)),
            *(pl.BlockSpec((mid, columns), lambda i, k=k: (k, 0)) for k in (0, 0, 1, 1)),
        ],
        out_specs=[wide, pl.BlockSpec((1, 8, block), lambda i: (i, 0, 0))],
        compiler_params=pltpu.CompilerParams(vmem_limit_bytes=32 * 1024 * 1024),
        cost_estimate=pl.CostEstimate(
            flops=2 * rows * columns * depth,
            bytes_accessed=8 * rows * columns,
            transcendentals=rows * columns,
        ),
    )(hidden_lanes[None], partial, states, up, down, up, down)


def on_device(hidden, head_weight, teacher_scores, token_ids):
    width = head_weight.shape[1]
    tok, voc = lax.axis_index("tok"), lax.axis_index("voc")
    yl, x = tok // NX, tok % NX
    yh, z, core = voc // (2 * NZ), voc // 2 % NZ, voc % 2
    rows = hidden.shape[0]
    half = rows // 2
    part = (width // LANES + 1) // 2 * LANES
    skip = width - part
    overlap = 2 * part - width

    give = lax.dynamic_slice_in_dim(head_weight, (1 - yl) * skip, part, 1)
    other = tok_move(give, Y_LO)
    keep = lax.dynamic_slice_in_dim(head_weight, yl * skip, part, 1)
    k_p, k_m = tok_move(keep, x_shift(1)), tok_move(keep, x_shift(-1))
    r_p, r_m = tok_move(other, x_shift(1)), tok_move(other, x_shift(-1))
    hidden_half = lax.dynamic_slice_in_dim(hidden, core * half, half, 0)
    hidden_half, _ = lax.optimization_barrier((hidden_half, other))
    near = tok_move(hidden_half, Y_LO)
    mid = keep.shape[0] // 2
    far = voc_move(near, CORE)
    up = jnp.concatenate([k_p[:mid], r_p[:mid]], 0)
    down = jnp.concatenate([k_m[mid:], r_m[mid:]], 0)
    up, down, _ = lax.optimization_barrier((up, down, near))
    up, down = tok_move(up, x_shift(1)), tok_move(down, x_shift(-1))
    first = core == 0

    order = [(a, k) for a in (yl, 1 - yl) for k in (0, 3, 1)] + [(yl, 2), (1 - yl, 2)]

    def arranged(block):
        return jnp.concatenate(
            [
                lax.dynamic_slice_in_dim(block, (a * NX + (x + k) % NX) * 2 * mid, 2 * mid, 1)
                for a, k in order
            ],
            axis=1,
        )

    states = jnp.concatenate(
        [
            arranged(hidden),
            arranged(jnp.where(first, near, far)),
            arranged(jnp.where(first, far, near)),
        ],
        axis=0,
    )

    top = jnp.max(teacher_scores, axis=1)
    mass = jnp.sum(jnp.exp(0.5 * (teacher_scores - top[:, None])), axis=1)

    def teacher_block(of_core, of_y):
        block = lax.dynamic_slice_in_dim(
            teacher_scores, of_core * width + of_y * skip, part, 1
        )
        return jnp.exp(0.5 * (block - top[:, None])).astype(BF16)

    def by_token(mine, swapped, axis):
        return jnp.concatenate(
            [
                jnp.where(first, a, b)
                for m, s in zip(mine, swapped)
                for a, b in ((m, s), (s, m))
            ],
            axis=axis,
        )

    tell = jnp.stack(
        [top, mass, lax.dynamic_slice_in_dim(token_ids, core * half, half, 0).astype(F32)]
    )
    give_t = jnp.concatenate([teacher_block(core, 1 - yl), teacher_block(1 - core, 1 - yl)], 0)
    given, _ = lax.optimization_barrier((tell, far))
    near_tell = tok_move(given, Y_LO)
    give_t, _ = lax.optimization_barrier((give_t, near_tell))
    near_t = tok_move(give_t, Y_LO)
    told = voc_move(jnp.concatenate([tell, near_tell], 1), CORE)
    told = by_token([tell, near_tell], [told[:, :half], told[:, half:]], 1)
    ids = told[2].astype(jnp.int32)
    early = jnp.concatenate([keep, k_p, k_m, other, r_p, r_m], axis=0)
    states, _ = lax.optimization_barrier((states, near_tell))
    logits = jnp.dot(
        states[:, : early.shape[0]], early, preferred_element_type=F32
    )
    def of_core(piece, c):
        groups = piece.reshape(piece.shape[0] // (2 * LANES), 2, LANES, part)
        return lax.dynamic_index_in_dim(groups, c, 1, False).reshape(-1, part)

    soon = (keep, k_p, k_m, other) + tuple(lax.optimization_barrier((r_p, r_m, near_tell))[:2])

    def packed(c):
        space = jnp.zeros((4 * LANES, part), BF16)
        return jnp.concatenate([of_core(w, c) for w in soon] + [space], 0)

    logits, up, down, head_far, head_near, near_t = lax.optimization_barrier(
        (logits, up, down, packed(1 - core), packed(core), near_t)
    )
    swap_t = voc_move(jnp.concatenate([teacher_block(1 - core, yl), near_t[half:]], 0), CORE)
    teacher = by_token(
        [teacher_block(core, yl), near_t[:half]], [swap_t[:half], swap_t[half:]], 0
    )
    logits, seen = finish_logits(yl * overlap, logits, states, up, down)
    up, down, _ = lax.optimization_barrier((up, down, seen))
    late = (up[:mid], down[:mid], up[mid:], down[mid:])

    def filled(head, c):
        rest = jnp.concatenate([of_core(w, c) for w in late], 0)
        return lax.dynamic_update_slice(head, rest, (head.shape[0] - rest.shape[0], 0))

    head_far = voc_move(filled(head_far, 1 - core), CORE)
    head_near = filled(head_near, core)
    lane = lax.broadcasted_iota(jnp.int32, logits.shape, 1)
    own = lane >= yl * overlap
    seen = jnp.concatenate([seen[0, :3], seen[1, :3]], axis=1)
    seen = merge([seen, voc_move(seen, CORE)])
    turned = jnp.concatenate([seen[:, rows:], seen[:, :rows]], axis=1)
    across = voc_move(jnp.concatenate([seen, told[:2]], 0), Y_HI)
    seen = merge([seen, tok_move(turned, Y_LO), across[:3], both_move(turned, Y_BOTH)])
    seen = jnp.concatenate([seen, merge([told[:2], across[3:]])], 0)

    def merge_all(parts):
        return jnp.concatenate(
            [merge([p[:3] for p in parts]), merge([p[3:] for p in parts])], 0
        )

    one, two = voc_move(seen, z_split(1)), voc_move(seen, z_split(2))
    pair = jnp.where(first, seen, merge_all([seen, one]))
    pair, head_near = lax.optimization_barrier((pair, head_near))
    three = voc_move(pair, z_split(3))
    none = jnp.zeros_like(seen[0])
    blank = jnp.stack([one[0], none, none, one[3], none])
    seen = merge_all([jnp.where(first, seen, blank), one, two, three])
    seen = merge_all([seen, voc_move(seen, CORE)])
    weight = 2.0 * LOSS_SCALE * jnp.exp(0.5 * (told[0] - seen[3])) / seen[4]

    soft = jnp.exp(0.5 * (logits - seen[0][:, None]))
    hit = lane + (voc * width + yl * skip) == ids[:, None]
    grad = (
        soft * (2.0 * LOSS_SCALE / seen[1])[:, None]
        + soft * soft * (CE_WEIGHT * LOSS_SCALE / seen[2])[:, None]
        - teacher.astype(F32) * weight[:, None]
        - jnp.where(hit, CE_WEIGHT * LOSS_SCALE, 0.0)
    )
    grad = jnp.where(own, grad, 0.0).astype(BF16)

    grad_far = voc_move(grad, CORE)

    def back(g, w):
        return lax.dot_general(g, w, (((1,), (1,)), ((), ())), preferred_element_type=F32)

    here = back(grad, head_near)
    grad_far, _ = lax.optimization_barrier((grad_far, here[:8, :LANES]))
    here = here + back(grad_far, head_far)

    def arrival(far_y, dx):
        far_y = far_y.astype(jnp.int32)
        near_x = jnp.where(dx == 0, 0, jnp.where(dx == NX - 1, 1, 2))
        return jnp.where(dx == 2, 6 + far_y, 3 * far_y + near_x)

    def chunk(k):
        to = (z + k) % NZ
        dx = (to // 2 - x) % NX
        cols = [
            (2 * arrival(h != yl, dx) + to % 2) * LANES for h in range(2)
        ]
        return jnp.concatenate(
            [lax.dynamic_slice_in_dim(here, a, LANES, 1) * SEND_SCALE for a in cols], 1
        )

    edge = chunk(4).astype(F16)
    up, down = (
        voc_move(edge[:rows], z_shift(1)),
        voc_move(edge[rows:], z_shift(-1)),
    )
    up = jnp.concatenate([chunk(3)[:rows] + up.astype(F32), chunk(3)[rows:]], 0)
    down = jnp.concatenate([chunk(-3)[:rows], chunk(-3)[rows:] + down.astype(F32)], 0)
    up, down = up.astype(F16), down.astype(F16)
    for k in (2, 1):
        up, down = voc_move(up, z_shift(1)), voc_move(down, z_shift(-1))
        up = (chunk(k) + up.astype(F32)).astype(F16)
        down = (chunk(-k) + down.astype(F32)).astype(F16)
    up, down = voc_move(up, z_shift(1)), voc_move(down, z_shift(-1))
    done = chunk(0) + up.astype(F32) + down.astype(F32)

    def quarter(of_mine, of_yh):
        block = done[:rows] if of_mine else done[rows:]
        return lax.dynamic_slice_in_dim(block, of_yh * LANES, LANES, 1)

    total = (
        quarter(True, yh)
        + tok_move(quarter(False, yh).astype(F16), Y_LO).astype(F32)
        + voc_move(quarter(True, 1 - yh).astype(F16), Y_HI).astype(F32)
        + both_move(quarter(False, 1 - yh).astype(F16), Y_BOTH).astype(F32)
    )
    return (total * (1.0 / SEND_SCALE)).astype(BF16)


def solution(mesh):
    return jax.shard_map(
        on_device,
        mesh=mesh,
        in_specs=(P("tok", None), P("tok", "voc"), P("tok", "voc"), P("tok")),
        out_specs=P("tok", "voc"),
        check_vma=False,
    )
```
